256 devices in a mesh: row: 4 (over y), col: 16 (over z, core), layer: 4 (over x).
Axes of the slice: x: 4, y: 4, z: 8, core: 2. Of those that a mesh axis runs over, the one named last changes fastest.
Arguments:
- matrix: float32 [4096, 4096], P('row', 'col'), may hold values from -6 to 6
- pattern: int32 [128, 128], P('row', 'col'), may hold values 0 or 1
- keep: int32 [128, 128], P('row', 'col'), may hold values 0 or 1
Outputs:
- update: float32 [4096, 4096], P(('row', 'layer'), 'col')
The draws below stay inside these ranges and needn't reach their ends.
All inputs are finite; a program needn't handle non-finite values. No bound on the sum of `pattern` or of `keep` on one device may be relied on, other than what follows from the above.
Results may differ from the reference program's by a relative error of at most 0.00005.
Values sent between devices are 32-bit elements; how exact they have to be, the bound alone decides.
No kernel may reach another device: no remote copies, remote signals or barrier semaphores. Data moves between devices by JAX's collectives and lax.ppermute only.
A program may use at most 64 MiB of HBM per device.

```python
import jax
import jax.numpy as jnp
from jax import lax

BS = 32
NB = 128
ORDER = 4096


def plant(entries, key, low, largest):
    longest = entries.shape.index(max(entries.shape))
    spots = []
    for shift in (0, 1):
        where = [jax.random.randint(jax.random.fold_in(key, axis), (), 0, length) for axis, length in enumerate(entries.shape)]
        where[longest] = (where[longest] + shift) % entries.shape[longest]
        spots.append(tuple(where))
    return entries.at[spots[0]].set(low).at[spots[1]].set(largest)


def shard_levels(rng, dims, shards, low, largest):
    def one(axis_at, blocks):
        steps = jax.random.uniform(jax.random.fold_in(jax.random.fold_in(rng, 6), axis_at), (blocks,), jnp.float32, low / len(shards), largest / len(shards))
        return jnp.repeat(jnp.exp(steps), dims[axis_at] // blocks).reshape((-1,) + (1,) * (len(dims) - axis_at - 1))

    gain = one(*shards[0])
    for cut in shards[1:]:
        gain = gain * one(*cut)
    return gain


def normal_values(key, shape, deviation, limit, shards=(), kind=jnp.bfloat16):
    entries = deviation * jax.random.normal(key, shape, jnp.float32)
    if shards:
        entries = entries * shard_levels(key, shape, shards, -0.22, 0.18)
    return jnp.clip(entries, -limit, limit).astype(kind)


def setup_inputs(seed: int = 0) -> dict:
    streams_of = jax.random.split(jax.random.key(seed), 4)
    return {
        "matrix": normal_values(streams_of[0], (ORDER, ORDER), 1.0, 6.0, ((0, 4), (1, 16)), jnp.float32),
        "pattern": plant((jax.random.randint(streams_of[1], (NB, NB), 0, 2) < 1).astype(jnp.int32), jax.random.fold_in(streams_of[1], 1), 0, 1),
        "keep": plant((jax.random.randint(streams_of[2], (NB, NB), 0, 4) < 3).astype(jnp.int32), jax.random.fold_in(streams_of[2], 1), 0, 1),
    }


def blockwise(values, flags):
    shaped = values.reshape(NB, BS, NB, BS) * flags.astype(jnp.float32)[:, None, :, None]
    return shaped.reshape(NB * BS, NB * BS)


def reference(matrix, pattern, keep):
    sparse = blockwise(matrix, pattern)
    square = jnp.dot(sparse, sparse, preferred_element_type=jnp.float32, precision=lax.Precision.HIGHEST)
    filtered = blockwise(square, keep)
    product = jnp.dot(sparse, filtered, preferred_element_type=jnp.float32, precision=lax.Precision.HIGHEST)
    factor = 0.72 / (NB * BS)
    return 1.5 * sparse - (0.5 * factor) * product
```

```python
import functools

import jax
import jax.numpy as jnp
from jax import lax
from jax.experimental import pallas as pl
from jax.experimental.pallas import tpu as pltpu
from jax.sharding import PartitionSpec as P

BS = 32
NB = 128
F32 = jnp.float32
BF16 = jnp.bfloat16
VMEM = pl.BlockSpec(memory_space=pltpu.VMEM)


def expand(flags):
    r, c = flags.shape
    up = lax.broadcasted_iota(jnp.int32, (r * BS, r), 0) // BS == lax.broadcasted_iota(jnp.int32, (r * BS, r), 1)
    out = lax.broadcasted_iota(jnp.int32, (c, c * BS), 1) // BS == lax.broadcasted_iota(jnp.int32, (c, c * BS), 0)
    tall = jnp.dot(up.astype(BF16), flags.astype(BF16), preferred_element_type=F32)
    return jnp.dot(tall.astype(BF16), out.astype(BF16), preferred_element_type=F32)


def prep_kernel(matrix, pattern, keep, a_out, b_out, own_out, mask_out, sparse, kept):
    level = lax.axis_index("layer")
    core = lax.rem(lax.axis_index("col"), 2)
    rows = matrix.shape[0]
    half = rows // 2
    sparse[...] = matrix[...] * expand(pattern[...].astype(F32))
    kept[...] = expand(keep[...].astype(F32))
    for q in range(4):
        there = pl.ds(pl.multiple_of(256 * q + 64 * level, 64), 64)
        b_out[q] = sparse[there, :]
        mask_out[q] = kept[there, :]
    own_out[...] = 1.5 * sparse[pl.ds(pl.multiple_of(256 * level, 256), 256), :]
    tile = pl.ds(pl.multiple_of(128 * (level // 2), 128), 128)
    odd = lax.rem(level, 2)
    flip = lax.rem(core + odd, 2)
    still = sparse[pl.ds(pl.multiple_of(half * flip, half), half), tile]
    moved = sparse[pl.ds(pl.multiple_of(half * (1 - flip), half), half), tile]
    lane = lax.broadcasted_iota(jnp.int32, (half, 128), 1) // 64
    a_out[...] = jnp.where(lane == odd, still, pltpu.roll(moved, 64, 1))


def split(value):
    high = value.astype(BF16)
    return high, (value - high.astype(F32)).astype(BF16)


def product(a_hi, a_lo, b_hi, b_lo):
    dot = functools.partial(jnp.dot, preferred_element_type=F32)
    return dot(a_hi, b_hi) + (dot(a_hi, b_lo) + dot(a_lo, b_hi))


def first_kernel(*refs):
    pieces, right = refs[:18], refs[18:22]
    a_hi, a_lo, c_out, b_hi, b_lo = refs[22:]
    z = lax.axis_index("col") // 2
    core = lax.rem(lax.axis_index("col"), 2)
    row = lax.axis_index("row")
    half = a_hi.shape[0] // 2
    lane = lax.broadcasted_iota(jnp.int32, (half, 128), 1) // 64

    def place(mine, other, shift):
        top = jnp.where(lane == core, mine, other)
        bottom = pltpu.roll(jnp.where(lane == core, other, mine), 64, 1)
        at = pl.ds(pl.multiple_of(128 * lax.rem(z + shift + 8, 8), 128), 128)
        for k, part in ((0, top), (1, bottom)):
            high, low = split(part)
            a_hi[pl.ds(half * k, half), at] = high
            a_lo[pl.ds(half * k, half), at] = low

    for n, shift in enumerate((0, -1, 1, -2, 2, -3, 3)):
        place(pieces[2 * n][...], pieces[2 * n + 1][...], shift)
    far = [jnp.concatenate([pieces[14 + k][...], pieces[16 + k][...]], 0) for k in (0, 1)]
    place(far[0], far[1], 4)
    for n, shift in enumerate((0, 1, 2, 3)):
        high, low = split(right[n][...].reshape(256, 256))
        at = pl.ds(pl.multiple_of(256 * lax.rem(row + shift, 4), 256), 256)
        b_hi[at, :] = high
        b_lo[at, :] = low
    total = product(a_hi[...], a_lo[...], b_hi[...], b_lo[...])
    for q in range(4):
        for level in range(4):
            c_out[level, q] = total[256 * q + 64 * level : 256 * q + 64 * level + 64]


def second_kernel(a_hi, a_lo, right, c_out):
    high, low = split(right[...].reshape(1024, 256))
    total = product(a_hi[...], a_lo[...], high, low)
    c_out[...] = total.reshape(4, 256, 256)


def shape(*dims, kind=F32):
    return jax.ShapeDtypeStruct(dims, kind)


def call(kernel, outs, ins, scratch=(), flops=0, moved=0):
    return pl.pallas_call(
        kernel,
        out_shape=outs,
        in_specs=[VMEM] * ins,
        out_specs=jax.tree.map(lambda _: VMEM, outs),
        scratch_shapes=list(scratch),
        compiler_params=pltpu.CompilerParams(vmem_limit_bytes=40 << 20),
        cost_estimate=pl.CostEstimate(flops=flops, bytes_accessed=moved, transcendentals=0),
    )


def shift_by(count, step):
    return [(i, (i + step) % count) for i in range(count)]


def local(matrix, pattern, keep):
    level = lax.axis_index("layer")
    piece, right, own, mask = call(
        prep_kernel,
        (shape(512, 128), shape(4, 64, 256), shape(256, 256), shape(4, 64, 256)),
        3,
        [pltpu.VMEM((1024, 256), F32), pltpu.VMEM((1024, 256), F32)],
        moved=2 << 20,
    )(matrix, pattern, keep)

    swap = lambda v: lax.ppermute(v, "col", [(i, i ^ 1) for i in range(16)])
    up = lambda v: lax.ppermute(v, "col", shift_by(16, 2))
    down = lambda v: lax.ppermute(v, "col", shift_by(16, -2))
    from_row = lambda v, d: lax.ppermute(v, "row", shift_by(4, -d))

    rights = [right] + [from_row(right, d) for d in (1, 2, 3)]
    got = [piece, swap(piece)]
    fwd = bwd = piece
    for step in range(3):
        fwd, bwd = up(fwd), down(bwd)
        got += [fwd, swap(fwd), bwd, swap(bwd)]
    fwd, bwd = up(fwd[:256]), down(bwd[256:])
    got += [fwd, swap(fwd), bwd, swap(bwd)]

    a_hi, a_lo, partial_value = call(
        first_kernel,
        (shape(1024, 1024, kind=BF16), shape(1024, 1024, kind=BF16), shape(4, 4, 64, 256)),
        22,
        [pltpu.VMEM((1024, 256), BF16), pltpu.VMEM((1024, 256), BF16)],
        flops=3 << 29,
        moved=9 << 20,
    )(*got, *rights)

    parts = lax.all_to_all(partial_value, "layer", 0, 0, tiled=True)
    mine = jnp.sum(parts, axis=0) * mask
    full = lax.all_to_all(jnp.broadcast_to(mine[None], (4, *mine.shape)), "row", 0, 0, tiled=True)
    partial_update = call(second_kernel, shape(4, 256, 256), 3, flops=3 << 29, moved=6 << 20)(a_hi, a_lo, full)
    summed = jnp.sum(lax.all_to_all(partial_update, "layer", 0, 0, tiled=True), axis=0)
    factor = 0.72 / (NB * BS)
    return own - 0.5 * factor * summed


def solution(mesh):
    placed = (P("row", "col"), P("row", "col"), P("row", "col"))
    return jax.shard_map(
        local, mesh=mesh, in_specs=placed, out_specs=P(("row", "layer"), "col"), check_vma=False
    )
```

```python
import functools

import jax
import jax.numpy as jnp
from jax import lax
from jax.experimental import pallas as pl
from jax.experimental.pallas import tpu as pltpu
from jax.sharding import PartitionSpec as P

BS = 32
NB = 128
F32 = jnp.float32
BF16 = jnp.bfloat16
VMEM = pl.BlockSpec(memory_space=pltpu.VMEM)


def expand(flags):
    c, r = flags.shape
    up = lax.broadcasted_iota(jnp.int32, (r * BS, r), 0) // BS == lax.broadcasted_iota(jnp.int32, (r * BS, r), 1)
    out = lax.broadcasted_iota(jnp.int32, (c, c * BS), 1) // BS == lax.broadcasted_iota(jnp.int32, (c, c * BS), 0)
    tall = lax.dot_general(
        up.astype(BF16), flags.astype(BF16), (((1,), (1,)), ((), ())), preferred_element_type=F32
    )
    return jnp.dot(tall.astype(BF16), out.astype(BF16), preferred_element_type=F32)


def prep_kernel(matrix, pattern, keep, a_out, b_out, own_out, mask_out, sparse, kept):
    level = lax.axis_index("layer")
    core = lax.rem(lax.axis_index("col"), 2)
    rows = matrix.shape[0]
    half = rows // 2
    sparse[...] = matrix[...] * expand(pattern[...].astype(F32))
    kept[...] = expand(keep[...].astype(F32))
    for q in range(4):
        there = pl.ds(pl.multiple_of(256 * q + 64 * level, 64), 64)
        b_out[q] = sparse[there, :]
        mask_out[q] = kept[there, :]
    own_out[...] = 1.5 * sparse[pl.ds(pl.multiple_of(256 * level, 256), 256), :]
    tile = pl.ds(pl.multiple_of(128 * (level // 2), 128), 128)
    odd = lax.rem(level, 2)
    flip = lax.rem(core + odd, 2)
    still = sparse[pl.ds(pl.multiple_of(half * flip, half), half), tile]
    moved = sparse[pl.ds(pl.multiple_of(half * (1 - flip), half), half), tile]
    lane = lax.broadcasted_iota(jnp.int32, (half, 128), 1) // 64
    a_out[...] = jnp.where(lane == odd, still, pltpu.roll(moved, 64, 1))


def split(value):
    high = value.astype(BF16)
    return high, (value - high.astype(F32)).astype(BF16)


def product(a_hi, a_lo, b_hi, b_lo):
    dot = functools.partial(jnp.dot, preferred_element_type=F32)
    return dot(a_hi, b_hi) + (dot(a_hi, b_lo) + dot(a_lo, b_hi))


def first_kernel(*refs):
    pieces, right = refs[:18], refs[18:22]
    a_hi, a_lo = refs[22:24]
    outs, (b_hi, b_lo, total) = refs[24:28], refs[28:]
    z = lax.axis_index("col") // 2
    sign = 1 - 2 * lax.rem(z, 2)
    level = lax.axis_index("layer")
    core = lax.rem(lax.axis_index("col"), 2)
    row = lax.axis_index("row")
    half = a_hi.shape[0] // 2
    lane = lax.broadcasted_iota(jnp.int32, (half, 128), 1) // 64

    def place(mine, other, shift):
        top = jnp.where(lane == core, mine, other)
        bottom = pltpu.roll(jnp.where(lane == core, other, mine), 64, 1)
        at = pl.ds(pl.multiple_of(128 * lax.rem(z + sign * shift + 8, 8), 128), 128)
        for k, part in ((0, top), (1, bottom)):
            high, low = split(part)
            a_hi[pl.ds(half * k, half), at] = high
            a_lo[pl.ds(half * k, half), at] = low

    for n, shift in enumerate((0, 1, -1, 2, -2, 3, -3)):
        place(pieces[2 * n][...], pieces[2 * n + 1][...], shift)
    far = [jnp.concatenate([pieces[14 + k][...], pieces[16 + k][...]], 0) for k in (0, 1)]
    place(far[0], far[1], 4)
    lay_right(right, b_hi, b_lo, row)
    total[...] = product(a_hi[...], a_lo[...], b_hi[...], b_lo[...])
    for n in range(4):
        for q in range(4):
            outs[n][q] = total[pl.ds(pl.multiple_of(256 * q + 64 * (level ^ n), 64), 64), :]


def lay_right(right, b_hi, b_lo, row):
    for n in range(4):
        high, low = split(right[n][...].reshape(256, 256))
        at = pl.ds(pl.multiple_of(256 * (row ^ n), 256), 256)
        b_hi[at, :] = high
        b_lo[at, :] = low


def second_kernel(a_hi, a_lo, *refs):
    right, outs, (b_hi, b_lo, total) = refs[:4], refs[4:8], refs[8:]
    level = lax.axis_index("layer")
    lay_right(right, b_hi, b_lo, lax.axis_index("row"))
    total[...] = product(a_hi[...], a_lo[...], b_hi[...], b_lo[...])
    for n in range(4):
        outs[n][...] = total[pl.ds(pl.multiple_of(256 * (level ^ n), 256), 256), :]


def shape(*dims, kind=F32):
    return jax.ShapeDtypeStruct(dims, kind)


def call(kernel, outs, ins, scratch=(), flops=0, moved=0):
    return pl.pallas_call(
        kernel,
        out_shape=outs,
        in_specs=[VMEM] * ins,
        out_specs=jax.tree.map(lambda _: VMEM, outs),
        scratch_shapes=list(scratch),
        compiler_params=pltpu.CompilerParams(vmem_limit_bytes=40 << 20),
        cost_estimate=pl.CostEstimate(flops=flops, bytes_accessed=moved, transcendentals=0),
    )


def swap_by(value, axis, step):
    return lax.ppermute(value, axis, [(i, i ^ step) for i in range(lax.axis_size(axis))])


def swap_next(value):
    pairs = []
    for i in range(16):
        z, core = divmod(i, 2)
        other = (z + (1 if z % 2 else -1)) % 8
        pairs.append((i, 2 * other + core))
    return lax.ppermute(value, "col", pairs)


def local(matrix, pattern, keep):
    piece, right, own, mask = call(
        prep_kernel,
        (shape(512, 128), shape(4, 64, 256), shape(256, 256), shape(4, 64, 256)),
        3,
        [pltpu.VMEM((1024, 256), F32), pltpu.VMEM((1024, 256), F32)],
        moved=2 << 20,
    )(matrix, pattern.T, keep.T)

    rights = [right] + [swap_by(right, "row", n) for n in (1, 2, 3)]
    both = lambda v: [v, swap_by(v, "col", 1)]
    got = both(piece)
    one = two = piece
    for step in range(3):
        one, two = swap_by(one, "col", 2), swap_next(two)
        got += both(one) + both(two)
        one, two = two, one
    one, two = swap_by(one[:256], "col", 2), swap_next(two[256:])
    got += both(one) + both(two)

    laid = [pltpu.VMEM((1024, 256), BF16), pltpu.VMEM((1024, 256), BF16), pltpu.VMEM((1024, 256), F32)]
    a_hi, a_lo, *parts = call(
        first_kernel,
        (shape(1024, 1024, kind=BF16), shape(1024, 1024, kind=BF16)) + (shape(4, 64, 256),) * 4,
        22,
        laid,
        flops=3 << 29,
        moved=9 << 20,
    )(*got, *rights)

    mine = summed(parts) * mask
    full = [mine] + [swap_by(mine, "row", n) for n in (1, 2, 3)]
    parts = call(second_kernel, (shape(256, 256),) * 4, 6, laid, flops=3 << 29, moved=6 << 20)(
        a_hi, a_lo, *full
    )
    factor = 0.72 / (NB * BS)
    return own - 0.5 * factor * summed(parts)


def summed(parts):
    total = parts[0]
    for n in (1, 2, 3):
        total = total + swap_by(parts[n], "layer", n)
    return total


def solution(mesh):
    placed = (P("row", "col"), P("row", "col"), P("row", "col"))
    return jax.shard_map(
        local, mesh=mesh, in_specs=placed, out_specs=P(("row", "layer"), "col"), check_vma=False
    )
```

```python
import functools

import jax
import jax.numpy as jnp
from jax import lax
from jax.experimental import pallas as pl
from jax.experimental.pallas import tpu as pltpu
from jax.sharding import PartitionSpec as P

BS = 32
NB = 128
F32 = jnp.float32
BF16 = jnp.bfloat16
VMEM = pl.BlockSpec(memory_space=pltpu.VMEM)
OFFS = (0, 1, -1, 2, -2, 3, -3, 4)


def shape(*dims, kind=F32):
    return jax.ShapeDtypeStruct(dims, kind)


def call(kernel, outs, scratch=(), flops=0, moved=0):
    def run(*args):
        return pl.pallas_call(
            kernel,
            out_shape=outs,
            in_specs=[VMEM] * len(args),
            out_specs=jax.tree.map(lambda _: VMEM, outs),
            scratch_shapes=list(scratch),
            compiler_params=pltpu.CompilerParams(vmem_limit_bytes=32 << 20),
            cost_estimate=pl.CostEstimate(flops=flops, bytes_accessed=moved, transcendentals=0),
        )(*args)

    return run


def aligned(start, length):
    return pl.ds(pl.multiple_of(start, length), length)


def place():
    col = lax.axis_index("col")
    z = col // 2
    return lax.axis_index("layer"), lax.axis_index("row"), z, lax.rem(col, 2), 1 - 2 * lax.rem(z, 2)


def expand(flags):
    c, r = flags.shape
    up = lax.broadcasted_iota(jnp.int32, (r * BS, r), 0) // BS == lax.broadcasted_iota(jnp.int32, (r * BS, r), 1)
    out = lax.broadcasted_iota(jnp.int32, (c, c * BS), 1) // BS == lax.broadcasted_iota(jnp.int32, (c, c * BS), 0)
    tall = lax.dot_general(
        up.astype(BF16), flags.astype(BF16), (((1,), (1,)), ((), ())), preferred_element_type=F32
    )
    return jnp.dot(tall.astype(BF16), out.astype(BF16), preferred_element_type=F32)


def prep_kernel(matrix, pattern, keep, piece, block, quarter, mask, kept):
    level = lax.axis_index("layer")
    block[...] = matrix[...] * expand(pattern[...].astype(F32))
    kept[...] = expand(keep[...].astype(F32))
    for h in range(2):
        there = aligned(512 * h + 128 * level, 128)
        piece[128 * h : 128 * h + 128, :] = block[there, :]
        mask[128 * h : 128 * h + 128, :] = kept[there, :]
    quarter[...] = block[aligned(256 * level, 256), :]


def split(value):
    high = value.astype(BF16)
    return high, (value - high.astype(F32)).astype(BF16)


def product(a_hi, a_lo, b_hi, b_lo):
    dot = functools.partial(jnp.dot, preferred_element_type=F32)
    return dot(a_hi, b_hi) + (dot(a_hi, b_lo) + dot(a_lo, b_hi))


def tile_of(pieces, index, which, half, target, core):
    lanes = aligned(128 * lax.rem(target, 2), 128)
    if OFFS[index] == 4:
        first, second = pieces[2 * index : 2 * index + 2], pieces[2 * index + 2 : 2 * index + 4]
        value = [jnp.where(half == 0, first[k][:, lanes], second[k][:, lanes]) for k in (0, 1)]
    else:
        rows = aligned(128 * half, 128)
        value = [pieces[2 * index + k][rows, lanes] for k in (0, 1)]
    return jnp.where(target // 2 == core, value[0], value[1])


def pack_kernel(indices, *refs):
    pieces, outs = refs[:-3], refs[-3:]
    level, _, _, core, _ = place()
    for n in (1, 2, 3):
        for m, index in enumerate(indices):
            shifted = [None] * (2 * indices[0]) + list(pieces)
            outs[n - 1][:, 128 * m : 128 * m + 128] = tile_of(shifted, index, m, core, level ^ n, core)


def lay_kernel(block, near, other, *refs):
    far, (b_hi, b_lo) = refs[:4], refs[4:]
    level, row, _, _, _ = place()

    def put(value, start):
        high, low = split(value)
        b_hi[aligned(start, value.shape[0]), :] = high
        b_lo[aligned(start, value.shape[0]), :] = low

    for n, ref in ((0, block), (1, near), (3, other)):
        put(ref[...], 1024 * (row ^ n))
    for n in range(4):
        put(far[n][...], 1024 * (row ^ 2) + 256 * (level ^ n))


def first_kernel(*refs):
    pieces, (b_hi, b_lo, mask, out) = refs[:18], refs[18:]
    _, _, z, core, sign = place()
    total = jnp.zeros((256, 256), F32)
    for n, off in enumerate(OFFS):
        for k in (0, 1):
            if off == 4:
                value = jnp.concatenate([pieces[2 * n + k][...], pieces[2 * n + 2 + k][...]], 0)
            else:
                value = pieces[2 * n + k][...]
            high, low = split(value)
            owner = 2 * lax.rem(z + sign * off + 8, 8) + (core + k - 2 * core * k)
            rows = aligned(256 * owner, 256)
            total += product(high, low, b_hi[rows, :], b_lo[rows, :])
    out[...] = total * mask[...]


def panel_kernel(*refs):
    pieces, bundles, (a_hi, a_lo) = refs[:18], refs[18:30], refs[30:]
    level, _, z, core, sign = place()

    def put(value, half, owner, off):
        high, low = split(value)
        rows = aligned(512 * half + 128 * owner, 128)
        lanes = aligned(128 * lax.rem(z + sign * off + 8, 8), 128)
        a_hi[rows, lanes] = high
        a_lo[rows, lanes] = low

    for index, off in enumerate(OFFS):
        for half in (0, 1):
            put(tile_of(pieces, index, 0, half, level, core), half, level, off)
    for n in (1, 2, 3):
        for part, offs in ((0, OFFS[:5]), (1, OFFS[5:])):
            mine, other = bundles[4 * (n - 1) + 2 * part : 4 * (n - 1) + 2 * part + 2]
            for m, off in enumerate(offs):
                lanes = slice(128 * m, 128 * m + 128)
                put(mine[:, lanes], core, level ^ n, off)
                put(other[:, lanes], 1 - core, level ^ n, off)


def second_kernel(a_hi, a_lo, *refs):
    right, outs, (b_hi, b_lo, total) = refs[:4], refs[4:8], refs[8:]
    level, row, _, _, _ = place()
    for n in range(4):
        high, low = split(right[n][...])
        b_hi[aligned(256 * (row ^ n), 256), :] = high
        b_lo[aligned(256 * (row ^ n), 256), :] = low
    total[...] = product(a_hi[...], a_lo[...], b_hi[...], b_lo[...])
    for n in range(4):
        outs[n][...] = total[aligned(256 * (level ^ n), 256), :]


def swap_by(value, axis, step):
    return lax.ppermute(value, axis, [(i, i ^ step) for i in range(lax.axis_size(axis))])


def swap_next(value):
    pairs = []
    for i in range(16):
        z, core = divmod(i, 2)
        other = (z + (1 if z % 2 else -1)) % 8
        pairs.append((i, 2 * other + core))
    return lax.ppermute(value, "col", pairs)


def both(value):
    return [value, swap_by(value, "col", 1)]


def exchanged(pieces, indices):
    lots = call(functools.partial(pack_kernel, indices), (shape(128, 128 * len(indices)),) * 3, moved=3 << 20)(*pieces)
    return [both(swap_by(lots[n - 1], "layer", n)) for n in (1, 2, 3)]


def local(matrix, pattern, keep):
    piece, block, quarter, mask = call(
        prep_kernel,
        (shape(256, 256), shape(1024, 256), shape(256, 256), shape(256, 256)),
        [pltpu.VMEM((1024, 256), F32)],
        moved=2 << 20,
    )(matrix, pattern.T, keep.T)

    near, other = swap_by(block, "row", 1), swap_by(block, "row", 3)
    far = swap_by(quarter, "row", 2)
    far = [far] + [swap_by(far, "layer", n) for n in (1, 2, 3)]

    got = both(piece)
    one = two = piece
    for step in range(3):
        one, two = swap_by(one, "col", 2), swap_next(two)
        got += both(one) + both(two)
        one, two = two, one
        if step == 1:
            early = exchanged(got, (0, 1, 2, 3, 4))
    one, two = swap_by(one[:128], "col", 2), swap_next(two[128:])
    got += both(one) + both(two)
    late = exchanged(got[10:], (5, 6, 7))

    wide = shape(4096, 256, kind=BF16)
    b_hi, b_lo = call(lay_kernel, (wide, wide), moved=8 << 20)(block, near, other, *far)
    mine = call(first_kernel, shape(256, 256), flops=3 << 29, moved=8 << 20)(*got, b_hi, b_lo, mask)
    full = [mine] + [swap_by(mine, "row", n) for n in (1, 2, 3)]

    square = shape(1024, 1024, kind=BF16)
    bundles = sum((early[n] + late[n] for n in range(3)), [])
    a_hi, a_lo = call(panel_kernel, (square, square), moved=8 << 20)(*got, *bundles)
    parts = call(
        second_kernel,
        (shape(256, 256),) * 4,
        [pltpu.VMEM((1024, 256), BF16), pltpu.VMEM((1024, 256), BF16), pltpu.VMEM((1024, 256), F32)],
        flops=3 << 29,
        moved=6 << 20,
    )(a_hi, a_lo, *full)
    total = parts[0]
    for n in (1, 2, 3):
        total = total + swap_by(parts[n], "layer", n)
    factor = 0.72 / (NB * BS)
    return 1.5 * quarter - 0.5 * factor * total


def solution(mesh):
    placed = (P("row", "col"), P("row", "col"), P("row", "col"))
    return jax.shard_map(
        local, mesh=mesh, in_specs=placed, out_specs=P(("row", "layer"), "col"), check_vma=False
    )
```

```python
import functools

import jax
import jax.numpy as jnp
from jax import lax
from jax.experimental import pallas as pl
from jax.experimental.pallas import tpu as pltpu
from jax.sharding import PartitionSpec as P

BS = 32
NB = 128
F32 = jnp.float32
BF16 = jnp.bfloat16
VMEM = pl.BlockSpec(memory_space=pltpu.VMEM)


def expand(flags):
    c, r = flags.shape
    up = lax.broadcasted_iota(jnp.int32, (r * BS, r), 0) // BS == lax.broadcasted_iota(jnp.int32, (r * BS, r), 1)
    out = lax.broadcasted_iota(jnp.int32, (c, c * BS), 1) // BS == lax.broadcasted_iota(jnp.int32, (c, c * BS), 0)
    tall = lax.dot_general(
        up.astype(BF16), flags.astype(BF16), (((1,), (1,)), ((), ())), preferred_element_type=F32
    )
    return jnp.dot(tall.astype(BF16), out.astype(BF16), preferred_element_type=F32)


def prep_kernel(matrix, pattern, a_out, b_out, own_out, sparse):
    level = lax.axis_index("layer")
    core = lax.rem(lax.axis_index("col"), 2)
    rows = matrix.shape[0]
    half = rows // 2
    sparse[...] = matrix[...] * expand(pattern[...].astype(F32))
    for q in range(4):
        b_out[q] = sparse[aligned(256 * q + 64 * level, 64), :]
    own_out[...] = 1.5 * sparse[aligned(256 * level, 256), :]
    tile = aligned(128 * (level // 2), 128)
    odd = lax.rem(level, 2)
    flip = lax.rem(core + odd, 2)
    still = sparse[aligned(half * flip, half), tile]
    moved = sparse[aligned(half * (1 - flip), half), tile]
    lane = lax.broadcasted_iota(jnp.int32, (half, 128), 1) // 64
    a_out[...] = jnp.where(lane == odd, still, pltpu.roll(moved, 64, 1))


def split(value):
    high = value.astype(BF16)
    return high, (value - high.astype(F32)).astype(BF16)


def product(a_hi, a_lo, b_hi, b_lo):
    dot = functools.partial(jnp.dot, preferred_element_type=F32)
    return dot(a_hi, b_hi) + (dot(a_hi, b_lo) + dot(a_lo, b_hi))


def put_piece(a_hi, a_lo, mine, other, shift):
    z = lax.axis_index("col") // 2
    core = lax.rem(lax.axis_index("col"), 2)
    sign = 1 - 2 * lax.rem(z, 2)
    half = a_hi.shape[0] // 2
    lane = lax.broadcasted_iota(jnp.int32, (half, 128), 1) // 64
    top = jnp.where(lane == core, mine, other)
    bottom = pltpu.roll(jnp.where(lane == core, other, mine), 64, 1)
    at = aligned(128 * lax.rem(z + sign * shift + 8, 8), 128)
    for k, part in ((0, top), (1, bottom)):
        high, low = split(part)
        a_hi[pl.ds(half * k, half), at] = high
        a_lo[pl.ds(half * k, half), at] = low


def lay_right(right, b_hi, b_lo):
    row = lax.axis_index("row")
    for n in range(4):
        value = right[n][...]
        high, low = split(value.reshape(256, value.shape[-1]))
        at = aligned(256 * (row ^ n), 256)
        b_hi[at, :] = high
        b_lo[at, :] = low


def gather_kernel(*refs):
    pieces, right, keep, (a_hi, a_lo, b_hi, b_lo, mask, kept) = refs[:10], refs[10:14], refs[14], refs[15:]
    level = lax.axis_index("layer")
    for n, shift in enumerate((0, 1, -1, 2, -2)):
        put_piece(a_hi, a_lo, pieces[2 * n][...], pieces[2 * n + 1][...], shift)
    lay_right(right, b_hi, b_lo)
    kept[...] = expand(keep[...].astype(F32))
    for q in range(4):
        mask[q] = kept[aligned(256 * q + 64 * level, 64), :]


def send_square(total, outs):
    level = lax.axis_index("layer")
    for n in range(4):
        for q in range(4):
            outs[n][q] = total[aligned(256 * q + 64 * (level ^ n), 64), :]


def first_kernel(*refs):
    pieces, (b_hi, b_lo, _, _), (a_hi, a_lo), outs, total = refs[:8], refs[8:12], refs[12:14], refs[14:18], refs[18]
    for n, shift in enumerate((3, -3)):
        put_piece(a_hi, a_lo, pieces[2 * n][...], pieces[2 * n + 1][...], shift)
    far = [jnp.concatenate([pieces[4 + k][...], pieces[6 + k][...]], 0) for k in (0, 1)]
    put_piece(a_hi, a_lo, far[0], far[1], 4)
    total[...] = product(a_hi[...], a_lo[...], b_hi[:, :128], b_lo[:, :128])
    send_square(total, outs)


def next_kernel(b_hi, b_lo, a_hi, a_lo, *refs):
    outs, total = refs[:4], refs[4]
    total[...] = product(a_hi[...], a_lo[...], b_hi[:, 128:], b_lo[:, 128:])
    send_square(total, outs)


def second_kernel(a_hi, a_lo, *refs):
    right, outs, (b_hi, b_lo, total) = refs[:4], refs[4:8], refs[8:]
    level = lax.axis_index("layer")
    lay_right(right, b_hi, b_lo)
    total[...] = product(a_hi[...], a_lo[...], b_hi[...], b_lo[...])
    for n in range(4):
        outs[n][...] = total[aligned(256 * (level ^ n), 256), :]


def aligned(start, length):
    return pl.ds(pl.multiple_of(start, length), length)


def call(kernel, outs, scratch=(), flops=0, moved=0, aliases={}):
    def run(*args):
        return pl.pallas_call(
            kernel,
            out_shape=outs,
            in_specs=[VMEM] * len(args),
            out_specs=jax.tree.map(lambda _: VMEM, outs),
            scratch_shapes=list(scratch),
            input_output_aliases=aliases,
            compiler_params=pltpu.CompilerParams(vmem_limit_bytes=32 << 20),
            cost_estimate=pl.CostEstimate(flops=flops, bytes_accessed=moved, transcendentals=0),
        )(*args)

    return run


def shape(*dims, kind=F32):
    return jax.ShapeDtypeStruct(dims, kind)


def swap_by(value, axis, step):
    return lax.ppermute(value, axis, [(i, i ^ step) for i in range(lax.axis_size(axis))])


def swap_next(value):
    pairs = []
    for i in range(16):
        z, core = divmod(i, 2)
        other = (z + (1 if z % 2 else -1)) % 8
        pairs.append((i, 2 * other + core))
    return lax.ppermute(value, "col", pairs)


def swap_beyond(value):
    pairs = []
    for i in range(16):
        z, core = divmod(i, 2)
        pairs.append((i, 2 * ((z + (2 if z % 4 > 1 else -2)) % 8) + core))
    return lax.ppermute(value, "col", pairs)


def local(matrix, pattern, keep):
    piece, right, own = call(
        prep_kernel,
        (shape(512, 128), shape(4, 64, 256), shape(256, 256)),
        [pltpu.VMEM((1024, 256), F32)],
        moved=2 << 20,
    )(matrix, pattern.T)

    rights = [right] + [swap_by(right, "row", n) for n in (1, 2, 3)]
    both = lambda v: [v, swap_by(v, "col", 1)]
    got = both(piece)
    one = two = piece
    for step in range(2):
        one, two = swap_by(one, "col", 2), swap_next(two)
        got += both(one) + both(two)
        one, two = two, one
    one, two, *rights[1:] = lax.optimization_barrier((one, two, *rights[1:]))
    z = lax.axis_index("col") // 2
    outer = lax.rem(z + 1, 4) < 2
    top = jnp.where(outer, one[:256], two[:256])
    bottom = jnp.where(outer, two[256:], one[256:])
    top, bottom = swap_by(top, "col", 4), swap_beyond(bottom)
    one, two = swap_by(one, "col", 2), swap_next(two)

    square, tall = shape(1024, 1024, kind=BF16), shape(1024, 256, kind=BF16)
    total = pltpu.VMEM((1024, 128), F32)
    a_hi, a_lo, b_hi, b_lo, mask = call(
        gather_kernel,
        (square, square, tall, tall, shape(4, 64, 256)),
        [pltpu.VMEM((1024, 256), F32)],
        moved=9 << 20,
    )(*got, *rights, keep.T)
    one, two, top, bottom, a_hi, a_lo = lax.optimization_barrier((one, two, top, bottom, a_hi, a_lo))
    far = both(one) + both(two) + both(top) + both(bottom)
    quarters = (shape(4, 64, 128),) * 4
    a_hi, a_lo, *first = call(
        first_kernel, (square, square) + quarters, [total], flops=3 << 28, moved=6 << 20, aliases={10: 0, 11: 1}
    )(*far, b_hi, b_lo, a_hi, a_lo)
    other = call(next_kernel, quarters, [total], flops=3 << 28, moved=6 << 20)(b_hi, b_lo, a_hi, a_lo)

    sums = []
    for side, parts in enumerate((first, other)):
        if side:
            *parts, _ = lax.optimization_barrier((*parts, mine))
        mine = summed(parts) * mask[:, :, 128 * side : 128 * side + 128]
        full = [mine] + [swap_by(mine, "row", n) for n in (1, 2, 3)]
        parts = call(
            second_kernel,
            (shape(256, 128),) * 4,
            [pltpu.VMEM((1024, 128), BF16), pltpu.VMEM((1024, 128), BF16), total],
            flops=3 << 28,
            moved=6 << 20,
        )(a_hi, a_lo, *full)
        sums.append(summed(parts))
    factor = 0.72 / (NB * BS)
    return own - 0.5 * factor * jnp.concatenate(sums, 1)


def summed(parts):
    total = parts[0]
    for n in (1, 2, 3):
        total = total + swap_by(parts[n], "layer", n)
    return total


def solution(mesh):
    placed = (P("row", "col"), P("row", "col"), P("row", "col"))
    return jax.shard_map(
        local, mesh=mesh, in_specs=placed, out_specs=P(("row", "layer"), "col"), check_vma=False
    )
```

```python
import functools

import jax
import jax.numpy as jnp
from jax import lax
from jax.experimental import pallas as pl
from jax.experimental.pallas import tpu as pltpu
from jax.sharding import PartitionSpec as P

BS = 32
NB = 128
F32 = jnp.float32
BF16 = jnp.bfloat16
VMEM = pl.BlockSpec(memory_space=pltpu.VMEM)
OFFS = (0, 1, -1, 2, -2, 3, -3, 4)


def expand(flags):
    c, r = flags.shape
    up = lax.broadcasted_iota(jnp.int32, (r * BS, r), 0) // BS == lax.broadcasted_iota(jnp.int32, (r * BS, r), 1)
    out = lax.broadcasted_iota(jnp.int32, (c, c * BS), 1) // BS == lax.broadcasted_iota(jnp.int32, (c, c * BS), 0)
    tall = lax.dot_general(
        up.astype(BF16), flags.astype(BF16), (((1,), (1,)), ((), ())), preferred_element_type=F32
    )
    return jnp.dot(tall.astype(BF16), out.astype(BF16), preferred_element_type=F32)


def prep_kernel(matrix, pattern, a_out, b_out, own_out, sparse, flags, sems):
    level = lax.axis_index("layer")
    core = lax.rem(lax.axis_index("col"), 2)
    rows = matrix.shape[0]
    half = rows // 2
    copies = [
        pltpu.make_async_copy(pattern, flags, sems.at[0]),
        pltpu.make_async_copy(matrix, sparse, sems.at[1]),
    ]
    for copy in copies:
        copy.start()
    copies[0].wait()
    wide = expand(flags[...].astype(F32))
    copies[1].wait()
    sparse[...] = sparse[...] * wide
    for q in range(4):
        b_out[64 * q : 64 * q + 64, :] = sparse[aligned(256 * q + 64 * level, 64), :]
    own_out[...] = 1.5 * sparse[aligned(256 * level, 256), :]
    tile = aligned(128 * (level // 2), 128)
    odd = lax.rem(level, 2)
    flip = lax.rem(core + odd, 2)
    still = sparse[aligned(half * flip, half), tile]
    moved = sparse[aligned(half * (1 - flip), half), tile]
    lane = lax.broadcasted_iota(jnp.int32, (half, 128), 1) // 64
    a_out[...] = jnp.where(lane == odd, still, pltpu.roll(moved, 64, 1))


def split(value):
    high = value.astype(BF16)
    return high, (value - high.astype(F32)).astype(BF16)


def product(a_hi, a_lo, b_hi, b_lo):
    dot = functools.partial(jnp.dot, preferred_element_type=F32)
    return dot(a_hi, b_hi) + (dot(a_hi, b_lo) + dot(a_lo, b_hi))


def put_piece(a_hi, a_lo, mine, other, shift):
    core = lax.rem(lax.axis_index("col"), 2)
    half = a_hi.shape[0] // 2
    lane = lax.broadcasted_iota(jnp.int32, (half, 128), 1) // 64
    top = jnp.where(lane == core, mine, other)
    bottom = pltpu.roll(jnp.where(lane == core, other, mine), 64, 1)
    at = slice(128 * OFFS.index(shift), 128 * OFFS.index(shift) + 128)
    for k, part in ((0, top), (1, bottom)):
        high, low = split(part)
        a_hi[pl.ds(half * k, half), at] = high
        a_lo[pl.ds(half * k, half), at] = low


def lay_right(right, b_hi, b_lo):
    row, z = lax.axis_index("row"), lax.axis_index("col") // 2
    sign = 1 - 2 * lax.rem(z, 2)
    for n in range(4):
        high, low = split(right[n][...])
        for k in (0, 1):
            off = lax.rem(sign * (2 * (row ^ n) + k - z) + 16, 8)
            index = jnp.where(off == 0, 0, jnp.where(off <= 4, 2 * off - 1, 16 - 2 * off))
            at = aligned(128 * index, 128)
            b_hi[at, :] = high[128 * k : 128 * k + 128]
            b_lo[at, :] = low[128 * k : 128 * k + 128]


def gather_kernel(*refs):
    pieces, right, keep, (a_hi, a_lo, b_hi, b_lo, mask, begun, kept) = refs[:10], refs[10:14], refs[14], refs[15:]
    level = lax.axis_index("layer")
    for n, shift in enumerate((0, 1, -1, 2, -2)):
        put_piece(a_hi, a_lo, pieces[2 * n][...], pieces[2 * n + 1][...], shift)
    lay_right(right, b_hi, b_lo)
    begun[...] = product(a_hi[:, :640], a_lo[:, :640], b_hi[:640, :], b_lo[:640, :])
    kept[...] = expand(keep[...].astype(F32))
    for q in range(4):
        mask[64 * q : 64 * q + 64, :] = kept[aligned(256 * q + 64 * level, 64), :]


def send_square(total, outs):
    level = lax.axis_index("layer")
    for n in range(4):
        for q in range(4):
            outs[n][64 * q : 64 * q + 64, :] = total[aligned(256 * q + 64 * (level ^ n), 64), :]


def first_kernel(*refs):
    pieces, (b_hi, b_lo, begun), (a_hi, a_lo), outs, total = refs[:8], refs[8:11], refs[13:15], refs[15:19], refs[19]
    for n, shift in enumerate((3, -3)):
        put_piece(a_hi, a_lo, pieces[2 * n][...], pieces[2 * n + 1][...], shift)
    far = [jnp.concatenate([pieces[4 + k][...], pieces[6 + k][...]], 0) for k in (0, 1)]
    put_piece(a_hi, a_lo, far[0], far[1], 4)
    rest = product(a_hi[:, 640:], a_lo[:, 640:], b_hi[640:, :128], b_lo[640:, :128])
    total[...] = begun[:, :128] + rest
    send_square(total, outs)


def next_kernel(b_hi, b_lo, begun, a_hi, a_lo, *refs):
    outs, total = refs[:4], refs[4]
    rest = product(a_hi[:, 640:], a_lo[:, 640:], b_hi[640:, 128:], b_lo[640:, 128:])
    total[...] = begun[:, 128:] + rest
    send_square(total, outs)


def second_kernel(a_hi, a_lo, *refs):
    right, outs, (b_hi, b_lo, total) = refs[:4], refs[4:8], refs[8:]
    level = lax.axis_index("layer")
    lay_right(right, b_hi, b_lo)
    total[...] = product(a_hi[...], a_lo[...], b_hi[...], b_lo[...])
    for n in range(4):
        outs[n][...] = total[aligned(256 * (level ^ n), 256), :]


def aligned(start, length):
    return pl.ds(pl.multiple_of(start, length), length)


def call(kernel, outs, scratch=(), flops=0, moved=0, aliases={}, place=pltpu.VMEM, limit=32 << 20):
    def run(*args):
        return pl.pallas_call(
            kernel,
            out_shape=outs,
            in_specs=[pl.BlockSpec(memory_space=place)] * len(args),
            out_specs=jax.tree.map(lambda _: VMEM, outs),
            scratch_shapes=list(scratch),
            input_output_aliases=aliases,
            compiler_params=pltpu.CompilerParams(vmem_limit_bytes=limit),
            cost_estimate=pl.CostEstimate(flops=flops, bytes_accessed=moved, transcendentals=0),
        )(*args)

    return run


def shape(*dims, kind=F32):
    return jax.ShapeDtypeStruct(dims, kind)


def swap_by(value, axis, step):
    return lax.ppermute(value, axis, [(i, i ^ step) for i in range(lax.axis_size(axis))])


def swap_next(value):
    pairs = []
    for i in range(16):
        z, core = divmod(i, 2)
        other = (z + (1 if z % 2 else -1)) % 8
        pairs.append((i, 2 * other + core))
    return lax.ppermute(value, "col", pairs)


def swap_beyond(value):
    pairs = []
    for i in range(16):
        z, core = divmod(i, 2)
        pairs.append((i, 2 * ((z + (2 if z % 4 > 1 else -2)) % 8) + core))
    return lax.ppermute(value, "col", pairs)


def local(matrix, pattern, keep):
    piece, right, own = call(
        prep_kernel,
        (shape(512, 128), shape(256, 256), shape(256, 256)),
        [pltpu.VMEM((1024, 256), F32), pltpu.VMEM((8, 32), jnp.int32), pltpu.SemaphoreType.DMA((2,))],
        moved=2 << 20,
        place=pltpu.HBM,
        limit=(64 << 20) - (5 << 18),
    )(matrix, pattern.T)

    rights = [right] + [swap_by(right, "row", n) for n in (1, 2, 3)]
    both = lambda v: [v, swap_by(v, "col", 1)]
    got = both(piece)
    one = two = piece
    for step in range(2):
        one, two = swap_by(one, "col", 2), swap_next(two)
        got += both(one) + both(two)
        one, two = two, one
    one, two, *rights[1:] = lax.optimization_barrier((one, two, *rights[1:]))
    z = lax.axis_index("col") // 2
    outer = lax.rem(z + 1, 4) < 2
    top = jnp.where(outer, one[:256], two[:256])
    bottom = jnp.where(outer, two[256:], one[256:])
    top, bottom = swap_by(top, "col", 4), swap_beyond(bottom)
    one, two = swap_by(one, "col", 2), swap_next(two)

    square, tall = shape(1024, 1024, kind=BF16), shape(1024, 256, kind=BF16)
    total = pltpu.VMEM((1024, 128), F32)
    a_hi, a_lo, b_hi, b_lo, mask, begun = call(
        gather_kernel,
        (square, square, tall, tall, shape(256, 256), shape(1024, 256)),
        [pltpu.VMEM((1024, 256), F32)],
        flops=15 << 26,
        moved=9 << 20,
    )(*got, *rights, keep.T)
    one, two, top, bottom, a_hi, a_lo = lax.optimization_barrier((one, two, top, bottom, a_hi, a_lo))
    far = both(one) + both(two) + both(top) + both(bottom)
    quarters = (shape(256, 128),) * 4
    a_hi, a_lo, *first = call(
        first_kernel, (square, square) + quarters, [total], flops=3 << 28, moved=6 << 20, aliases={11: 0, 12: 1}
    )(*far, b_hi, b_lo, begun, a_hi, a_lo)
    other = call(next_kernel, quarters, [total], flops=3 << 28, moved=6 << 20)(b_hi, b_lo, begun, a_hi, a_lo)

    sums = []
    for side, parts in enumerate((first, other)):
        if side:
            *parts, _ = lax.optimization_barrier((*parts, mine))
        mine = summed(parts) * mask[:, 128 * side : 128 * side + 128]
        full = [mine] + [swap_by(mine, "row", n) for n in (1, 2, 3)]
        parts = call(
            second_kernel,
            (shape(256, 128),) * 4,
            [pltpu.VMEM((1024, 128), BF16), pltpu.VMEM((1024, 128), BF16), total],
            flops=3 << 28,
            moved=6 << 20,
        )(a_hi, a_lo, *full)
        sums.append(summed(parts))
    factor = 0.72 / (NB * BS)
    return own - 0.5 * factor * jnp.concatenate(sums, 1)


def summed(parts):
    total = parts[0]
    for n in (1, 3, 2):
        total = total + swap_by(parts[n], "layer", n)
    return total


def solution(mesh):
    placed = (P("row", "col"), P("row", "col"), P("row", "col"))
    return jax.shard_map(
        local, mesh=mesh, in_specs=placed, out_specs=P(("row", "layer"), "col"), check_vma=False
    )
```

```python
import functools

import jax
import jax.numpy as jnp
from jax import lax
from jax.experimental import pallas as pl
from jax.experimental.pallas import tpu as pltpu
from jax.sharding import PartitionSpec as P

BS = 32
NB = 128
F32 = jnp.float32
BF16 = jnp.bfloat16
VMEM = pl.BlockSpec(memory_space=pltpu.VMEM)
OFFS = (0, 1, -1, 2, -2, 3, -3, 4)


def expand(flags):
    c, r = flags.shape
    up = lax.broadcasted_iota(jnp.int32, (r * BS, r), 0) // BS == lax.broadcasted_iota(jnp.int32, (r * BS, r), 1)
    out = lax.broadcasted_iota(jnp.int32, (c, c * BS), 1) // BS == lax.broadcasted_iota(jnp.int32, (c, c * BS), 0)
    tall = lax.dot_general(
        up.astype(BF16), flags.astype(BF16), (((1,), (1,)), ((), ())), preferred_element_type=F32
    )
    return jnp.dot(tall.astype(BF16), out.astype(BF16), preferred_element_type=F32)


def prep_kernel(matrix, pattern, a_out, b_out, own_out, sparse, flags, sems):
    level = lax.axis_index("layer")
    core = lax.rem(lax.axis_index("col"), 2)
    rows = matrix.shape[0]
    half = rows // 2
    copies = [pltpu.make_async_copy(pattern, flags, sems.at[4])]
    for q in range(4):
        here = pl.ds(256 * q, 256)
        copies.append(pltpu.make_async_copy(matrix.at[here, :], sparse.at[here, :], sems.at[q]))
    for copy in copies:
        copy.start()
    copies[0].wait()
    wide = expand(flags[...].astype(F32))
    for q in range(4):
        here = slice(256 * q, 256 * q + 256)
        copies[1 + q].wait()
        sparse[here, :] = sparse[here, :] * wide[here, :]
        b_out[64 * q : 64 * q + 64, :] = sparse[aligned(256 * q + 64 * level, 64), :]
    own_out[...] = 1.5 * sparse[aligned(256 * level, 256), :]
    tile = aligned(128 * (level // 2), 128)
    odd = lax.rem(level, 2)
    flip = lax.rem(core + odd, 2)
    still = sparse[aligned(half * flip, half), tile]
    moved = sparse[aligned(half * (1 - flip), half), tile]
    lane = lax.broadcasted_iota(jnp.int32, (half, 128), 1) // 64
    a_out[...] = jnp.where(lane == odd, still, pltpu.roll(moved, 64, 1))


def split(value):
    high = value.astype(BF16)
    return high, (value - high.astype(F32)).astype(BF16)


def product(a_hi, a_lo, b_hi, b_lo):
    dot = functools.partial(jnp.dot, preferred_element_type=F32)
    return dot(a_hi, b_hi) + (dot(a_hi, b_lo) + dot(a_lo, b_hi))


def half_product(a_hi, a_lo, b_hi, b_lo):
    dot = functools.partial(jnp.dot, preferred_element_type=F32)
    both = dot(a_hi, jnp.concatenate([b_hi, b_lo], 1))
    return both[:, :128] + (both[:, 128:] + dot(a_lo, b_hi))


def put_piece(a_hi, a_lo, mine, other, shift):
    core = lax.rem(lax.axis_index("col"), 2)
    half = a_hi.shape[0] // 2
    lane = lax.broadcasted_iota(jnp.int32, (half, 128), 1) // 64
    top = jnp.where(lane == core, mine, other)
    bottom = pltpu.roll(jnp.where(lane == core, other, mine), 64, 1)
    at = slice(128 * OFFS.index(shift), 128 * OFFS.index(shift) + 128)
    for k, part in ((0, top), (1, bottom)):
        high, low = split(part)
        a_hi[pl.ds(half * k, half), at] = high
        a_lo[pl.ds(half * k, half), at] = low


def lay_right(right, b_hi, b_lo):
    row, z = lax.axis_index("row"), lax.axis_index("col") // 2
    sign = 1 - 2 * lax.rem(z, 2)
    for n in range(4):
        high, low = split(right[n][...])
        for k in (0, 1):
            off = lax.rem(sign * (2 * (row ^ n) + k - z) + 16, 8)
            index = jnp.where(off == 0, 0, jnp.where(off <= 4, 2 * off - 1, 16 - 2 * off))
            at = aligned(128 * index, 128)
            b_hi[at, :] = high[128 * k : 128 * k + 128]
            b_lo[at, :] = low[128 * k : 128 * k + 128]


def gather_kernel(*refs):
    pieces, right, keep, (a_hi, a_lo, b_hi, b_lo, mask, begun, kept) = refs[:10], refs[10:14], refs[14], refs[15:]
    level = lax.axis_index("layer")
    for n, shift in enumerate((0, 1, -1, 2, -2)):
        put_piece(a_hi, a_lo, pieces[2 * n][...], pieces[2 * n + 1][...], shift)
    lay_right(right, b_hi, b_lo)
    begun[...] = product(a_hi[:, :640], a_lo[:, :640], b_hi[:640, :], b_lo[:640, :])
    kept[...] = expand(keep[...].astype(F32))
    for q in range(4):
        mask[64 * q : 64 * q + 64, :] = kept[aligned(256 * q + 64 * level, 64), :]


def send_square(total, outs):
    level = lax.axis_index("layer")
    for n in range(4):
        for q in range(4):
            outs[n][64 * q : 64 * q + 64, :] = total[aligned(256 * q + 64 * (level ^ n), 64), :]


def first_kernel(*refs):
    pieces, (b_hi, b_lo, begun), (a_hi, a_lo), outs, total = refs[:8], refs[8:11], refs[13:15], refs[15:19], refs[19]
    for n, shift in enumerate((3, -3)):
        put_piece(a_hi, a_lo, pieces[2 * n][...], pieces[2 * n + 1][...], shift)
    far = [jnp.concatenate([pieces[4 + k][...], pieces[6 + k][...]], 0) for k in (0, 1)]
    put_piece(a_hi, a_lo, far[0], far[1], 4)
    rest = half_product(a_hi[:, 640:], a_lo[:, 640:], b_hi[640:, :128], b_lo[640:, :128])
    total[...] = begun[:, :128] + rest
    send_square(total, outs)


def next_kernel(b_hi, b_lo, begun, a_hi, a_lo, *refs):
    outs, total = refs[:4], refs[4]
    rest = half_product(a_hi[:, 640:], a_lo[:, 640:], b_hi[640:, 128:], b_lo[640:, 128:])
    total[...] = begun[:, 128:] + rest
    send_square(total, outs)


def second_kernel(a_hi, a_lo, *refs):
    right, outs, (b_hi, b_lo, total) = refs[:4], refs[4:8], refs[8:]
    level = lax.axis_index("layer")
    lay_right(right, b_hi, b_lo)
    total[...] = half_product(a_hi[...], a_lo[...], b_hi[...], b_lo[...])
    for n in range(4):
        outs[n][...] = total[aligned(256 * (level ^ n), 256), :]


def aligned(start, length):
    return pl.ds(pl.multiple_of(start, length), length)


def call(kernel, outs, scratch=(), flops=0, moved=0, aliases={}, place=pltpu.VMEM, limit=32 << 20):
    def run(*args):
        return pl.pallas_call(
            kernel,
            out_shape=outs,
            in_specs=[pl.BlockSpec(memory_space=place)] * len(args),
            out_specs=jax.tree.map(lambda _: VMEM, outs),
            scratch_shapes=list(scratch),
            input_output_aliases=aliases,
            compiler_params=pltpu.CompilerParams(vmem_limit_bytes=limit),
            cost_estimate=pl.CostEstimate(flops=flops, bytes_accessed=moved, transcendentals=0),
        )(*args)

    return run


def shape(*dims, kind=F32):
    return jax.ShapeDtypeStruct(dims, kind)


def swap_by(value, axis, step):
    return lax.ppermute(value, axis, [(i, i ^ step) for i in range(lax.axis_size(axis))])


def swap_next(value):
    pairs = []
    for i in range(16):
        z, core = divmod(i, 2)
        other = (z + (1 if z % 2 else -1)) % 8
        pairs.append((i, 2 * other + core))
    return lax.ppermute(value, "col", pairs)


def swap_beyond(value):
    pairs = []
    for i in range(16):
        z, core = divmod(i, 2)
        pairs.append((i, 2 * ((z + (2 if z % 4 > 1 else -2)) % 8) + core))
    return lax.ppermute(value, "col", pairs)


def local(matrix, pattern, keep):
    piece, right, own = call(
        prep_kernel,
        (shape(512, 128), shape(256, 256), shape(256, 256)),
        [pltpu.VMEM((1024, 256), F32), pltpu.VMEM((8, 32), jnp.int32), pltpu.SemaphoreType.DMA((5,))],
        moved=2 << 20,
        place=pltpu.HBM,
        limit=(64 << 20) - (5 << 18),
    )(matrix, pattern.T)

    rights = [right] + [swap_by(right, "row", n) for n in (1, 2, 3)]
    both = lambda v: [v, swap_by(v, "col", 1)]
    got = both(piece)
    one = two = piece
    for step in range(2):
        one, two = swap_by(one, "col", 2), swap_next(two)
        got += both(one) + both(two)
        one, two = two, one
    one, two, *rights[1:] = lax.optimization_barrier((one, two, *rights[1:]))
    z = lax.axis_index("col") // 2
    outer = lax.rem(z + 1, 4) < 2
    top = jnp.where(outer, one[:256], two[:256])
    bottom = jnp.where(outer, two[256:], one[256:])
    top, bottom = swap_by(top, "col", 4), swap_beyond(bottom)
    one, two = swap_by(one, "col", 2), swap_next(two)

    square, tall = shape(1024, 1024, kind=BF16), shape(1024, 256, kind=BF16)
    total = pltpu.VMEM((1024, 128), F32)
    a_hi, a_lo, b_hi, b_lo, mask, begun = call(
        gather_kernel,
        (square, square, tall, tall, shape(256, 256), shape(1024, 256)),
        [pltpu.VMEM((1024, 256), F32)],
        flops=15 << 26,
        moved=9 << 20,
    )(*got, *rights, keep.T)
    one, two, top, bottom, a_hi, a_lo = lax.optimization_barrier((one, two, top, bottom, a_hi, a_lo))
    far = both(one) + both(two) + both(top) + both(bottom)
    quarters = (shape(256, 128),) * 4
    a_hi, a_lo, *first = call(
        first_kernel, (square, square) + quarters, [total], flops=3 << 28, moved=6 << 20, aliases={11: 0, 12: 1}
    )(*far, b_hi, b_lo, begun, a_hi, a_lo)
    other = call(next_kernel, quarters, [total], flops=3 << 28, moved=6 << 20)(b_hi, b_lo, begun, a_hi, a_lo)

    sums = []
    came = {}
    for side, parts in enumerate((first, other)):
        if side:
            *parts, _ = lax.optimization_barrier((*parts, came[1]))
        mine = summed(parts, came)
        if side:
            mine, _ = lax.optimization_barrier((mine, full[3]))
        mine = mine * mask[:, 128 * side : 128 * side + 128]
        full = [mine] + [swap_by(mine, "row", n) for n in (1, 2, 3)]
        parts = call(
            second_kernel,
            (shape(256, 128),) * 4,
            [pltpu.VMEM((1024, 128), BF16), pltpu.VMEM((1024, 128), BF16), total],
            flops=3 << 28,
            moved=6 << 20,
        )(a_hi, a_lo, *full)
        sums.append(summed(parts, {}))
    factor = 0.72 / (NB * BS)
    return own - 0.5 * factor * jnp.concatenate(sums, 1)


def summed(parts, came):
    total = parts[0]
    for n in (1, 3, 2):
        came[n] = swap_by(parts[n], "layer", n)
        total = total + came[n]
    return total


def solution(mesh):
    placed = (P("row", "col"), P("row", "col"), P("row", "col"))
    return jax.shard_map(
        local, mesh=mesh, in_specs=placed, out_specs=P(("row", "layer"), "col"), check_vma=False
    )
```

```python
import functools

import jax
import jax.numpy as jnp
from jax import lax
from jax.experimental import pallas as pl
from jax.experimental.pallas import tpu as pltpu
from jax.sharding import PartitionSpec as P

BS = 32
NB = 128
F32 = jnp.float32
BF16 = jnp.bfloat16
VMEM = pl.BlockSpec(memory_space=pltpu.VMEM)
OFFS = (0, 1, -1, 2, -2, 3, -3, 4)


def widen(flags):
    c = flags.shape[0]
    out = lax.broadcasted_iota(jnp.int32, (c, c * BS), 1) // BS == lax.broadcasted_iota(jnp.int32, (c, c * BS), 0)
    return lax.dot_general(
        flags.astype(BF16), out.astype(BF16), (((0,), (0,)), ((), ())), preferred_element_type=F32
    )


def prep_kernel(matrix, pattern, a_out, b_out, own_out, sparse, flags, sems):
    level = lax.axis_index("layer")
    core = lax.rem(lax.axis_index("col"), 2)
    rows = matrix.shape[0]
    half = rows // 2
    copies = [pltpu.make_async_copy(pattern, flags, sems.at[4])]
    for q in range(4):
        here = pl.ds(256 * q, 256)
        copies.append(pltpu.make_async_copy(matrix.at[here, :], sparse.at[here, :], sems.at[q]))
    for copy in copies:
        copy.start()
    copies[0].wait()
    wide = widen(flags[...].astype(F32))
    for q in range(4):
        copies[1 + q].wait()
        for r in range(8 * q, 8 * q + 8):
            here = slice(BS * r, BS * r + BS)
            sparse[here, :] = sparse[here, :] * wide[r : r + 1, :]
        b_out[64 * q : 64 * q + 64, :] = sparse[aligned(256 * q + 64 * level, 64), :]
    own_out[...] = 1.5 * sparse[aligned(256 * level, 256), :]
    tile = aligned(128 * (level // 2), 128)
    odd = lax.rem(level, 2)
    flip = lax.rem(core + odd, 2)
    still = sparse[aligned(half * flip, half), tile]
    moved = sparse[aligned(half * (1 - flip), half), tile]
    lane = lax.broadcasted_iota(jnp.int32, (half, 128), 1) // 64
    a_out[...] = jnp.where(lane == odd, still, pltpu.roll(moved, 64, 1))


def split(value):
    high = value.astype(BF16)
    return high, (value - high.astype(F32)).astype(BF16)


def product(a_hi, a_lo, b_hi, b_lo):
    dot = functools.partial(jnp.dot, preferred_element_type=F32)
    return dot(a_hi, b_hi) + (dot(a_hi, b_lo) + dot(a_lo, b_hi))


def half_product(a_hi, a_lo, b_hi, b_lo):
    dot = functools.partial(jnp.dot, preferred_element_type=F32)
    both = dot(a_hi, jnp.concatenate([b_hi, b_lo], 1))
    return both[:, :128] + (both[:, 128:] + dot(a_lo, b_hi))


def put_piece(a_hi, a_lo, mine, other, shift):
    core = lax.rem(lax.axis_index("col"), 2)
    half = a_hi.shape[0] // 2
    lane = lax.broadcasted_iota(jnp.int32, (half, 128), 1) // 64
    top = jnp.where(lane == core, mine, other)
    bottom = pltpu.roll(jnp.where(lane == core, other, mine), 64, 1)
    at = slice(128 * OFFS.index(shift), 128 * OFFS.index(shift) + 128)
    for k, part in ((0, top), (1, bottom)):
        high, low = split(part)
        a_hi[pl.ds(half * k, half), at] = high
        a_lo[pl.ds(half * k, half), at] = low


def lay_right(right, b_hi, b_lo):
    row, z = lax.axis_index("row"), lax.axis_index("col") // 2
    sign = 1 - 2 * lax.rem(z, 2)
    for n in range(4):
        high, low = split(right[n][...])
        for k in (0, 1):
            off = lax.rem(sign * (2 * (row ^ n) + k - z) + 16, 8)
            index = jnp.where(off == 0, 0, jnp.where(off <= 4, 2 * off - 1, 16 - 2 * off))
            at = aligned(128 * index, 128)
            b_hi[at, :] = high[128 * k : 128 * k + 128]
            b_lo[at, :] = low[128 * k : 128 * k + 128]


def gather_kernel(*refs):
    pieces, right, keep, (a_hi, a_lo, b_hi, b_lo, mask, begun, kept) = refs[:10], refs[10:14], refs[14], refs[15:]
    level = lax.axis_index("layer")
    for n, shift in enumerate((0, 1, -1, 2, -2)):
        put_piece(a_hi, a_lo, pieces[2 * n][...], pieces[2 * n + 1][...], shift)
    lay_right(right, b_hi, b_lo)
    begun[...] = product(a_hi[:, :640], a_lo[:, :640], b_hi[:640, :], b_lo[:640, :])
    wide = widen(keep[...].astype(F32))
    for r in range(32):
        kept[BS * r : BS * r + BS, :] = jnp.broadcast_to(wide[r : r + 1, :], (BS, 256))
    for q in range(4):
        mask[64 * q : 64 * q + 64, :] = kept[aligned(256 * q + 64 * level, 64), :]


def send_square(total, outs):
    level = lax.axis_index("layer")
    for n in range(4):
        for q in range(4):
            outs[n][64 * q : 64 * q + 64, :] = total[aligned(256 * q + 64 * (level ^ n), 64), :]


def first_kernel(*refs):
    pieces, (b_hi, b_lo, begun), (a_hi, a_lo), outs, total = refs[:8], refs[8:11], refs[13:15], refs[15:19], refs[19]
    for n, shift in enumerate((3, -3)):
        put_piece(a_hi, a_lo, pieces[2 * n][...], pieces[2 * n + 1][...], shift)
    far = [jnp.concatenate([pieces[4 + k][...], pieces[6 + k][...]], 0) for k in (0, 1)]
    put_piece(a_hi, a_lo, far[0], far[1], 4)
    rest = half_product(a_hi[:, 640:], a_lo[:, 640:], b_hi[640:, :128], b_lo[640:, :128])
    total[...] = begun[:, :128] + rest
    send_square(total, outs)


def next_kernel(b_hi, b_lo, begun, a_hi, a_lo, *refs):
    outs, total = refs[:4], refs[4]
    rest = half_product(a_hi[:, 640:], a_lo[:, 640:], b_hi[640:, 128:], b_lo[640:, 128:])
    total[...] = begun[:, 128:] + rest
    send_square(total, outs)


def second_kernel(a_hi, a_lo, *refs):
    right, outs, (b_hi, b_lo, total) = refs[:4], refs[4:8], refs[8:]
    level = lax.axis_index("layer")
    lay_right(right, b_hi, b_lo)
    total[...] = half_product(a_hi[...], a_lo[...], b_hi[...], b_lo[...])
    for n in range(4):
        outs[n][...] = total[aligned(256 * (level ^ n), 256), :]


def aligned(start, length):
    return pl.ds(pl.multiple_of(start, length), length)


def call(kernel, outs, scratch=(), flops=0, moved=0, aliases={}, place=pltpu.VMEM, limit=32 << 20):
    def run(*args):
        return pl.pallas_call(
            kernel,
            out_shape=outs,
            in_specs=[pl.BlockSpec(memory_space=place)] * len(args),
            out_specs=jax.tree.map(lambda _: VMEM, outs),
            scratch_shapes=list(scratch),
            input_output_aliases=aliases,
            compiler_params=pltpu.CompilerParams(vmem_limit_bytes=limit),
            cost_estimate=pl.CostEstimate(flops=flops, bytes_accessed=moved, transcendentals=0),
        )(*args)

    return run


def shape(*dims, kind=F32):
    return jax.ShapeDtypeStruct(dims, kind)


def swap_by(value, axis, step):
    return lax.ppermute(value, axis, [(i, i ^ step) for i in range(lax.axis_size(axis))])


def swap_next(value):
    pairs = []
    for i in range(16):
        z, core = divmod(i, 2)
        other = (z + (1 if z % 2 else -1)) % 8
        pairs.append((i, 2 * other + core))
    return lax.ppermute(value, "col", pairs)


def swap_beyond(value):
    pairs = []
    for i in range(16):
        z, core = divmod(i, 2)
        pairs.append((i, 2 * ((z + (2 if z % 4 > 1 else -2)) % 8) + core))
    return lax.ppermute(value, "col", pairs)


def local(matrix, pattern, keep):
    piece, right, own = call(
        prep_kernel,
        (shape(512, 128), shape(256, 256), shape(256, 256)),
        [pltpu.VMEM((1024, 256), F32), pltpu.VMEM((8, 32), jnp.int32), pltpu.SemaphoreType.DMA((5,))],
        moved=2 << 20,
        place=pltpu.HBM,
        limit=(64 << 20) - (5 << 18),
    )(matrix, pattern.T)

    rights = [right] + [swap_by(right, "row", n) for n in (1, 2, 3)]
    both = lambda v: [v, swap_by(v, "col", 1)]
    got = both(piece)
    one = two = piece
    for step in range(2):
        one, two = swap_by(one, "col", 2), swap_next(two)
        got += both(one) + both(two)
        one, two = two, one
    one, two, *rights[1:] = lax.optimization_barrier((one, two, *rights[1:]))
    z = lax.axis_index("col") // 2
    outer = lax.rem(z + 1, 4) < 2
    top = jnp.where(outer, one[:256], two[:256])
    bottom = jnp.where(outer, two[256:], one[256:])
    top, bottom = swap_by(top, "col", 4), swap_beyond(bottom)
    one, two = swap_by(one, "col", 2), swap_next(two)

    square, tall = shape(1024, 1024, kind=BF16), shape(1024, 256, kind=BF16)
    total = pltpu.VMEM((1024, 128), F32)
    a_hi, a_lo, b_hi, b_lo, mask, begun = call(
        gather_kernel,
        (square, square, tall, tall, shape(256, 256), shape(1024, 256)),
        [pltpu.VMEM((1024, 256), F32)],
        flops=15 << 26,
        moved=9 << 20,
    )(*got, *rights, keep.T)
    one, two, top, bottom, a_hi, a_lo = lax.optimization_barrier((one, two, top, bottom, a_hi, a_lo))
    far = both(one) + both(two) + both(top) + both(bottom)
    quarters = (shape(256, 128),) * 4
    a_hi, a_lo, *first = call(
        first_kernel, (square, square) + quarters, [total], flops=3 << 28, moved=6 << 20, aliases={11: 0, 12: 1}
    )(*far, b_hi, b_lo, begun, a_hi, a_lo)
    other = call(next_kernel, quarters, [total], flops=3 << 28, moved=6 << 20)(b_hi, b_lo, begun, a_hi, a_lo)

    sums = []
    came = {}
    for side, parts in enumerate((first, other)):
        if side:
            *parts, _ = lax.optimization_barrier((*parts, came[1]))
        mine = summed(parts, came, mine if side else None)
        mine = mine * mask[:, 128 * side : 128 * side + 128]
        full = [mine] + [swap_by(mine, "row", n) for n in (1, 2, 3)]
        parts = call(
            second_kernel,
            (shape(256, 128),) * 4,
            [pltpu.VMEM((1024, 128), BF16), pltpu.VMEM((1024, 128), BF16), total],
            flops=3 << 28,
            moved=6 << 20,
        )(a_hi, a_lo, *full)
        sums.append(summed(parts, {}))
    factor = 0.72 / (NB * BS)
    return own - 0.5 * factor * jnp.concatenate(sums, 1)


def summed(parts, came, after=None):
    total = parts[0]
    for n in (1, 3, 2):
        came[n] = swap_by(parts[n], "layer", n)
        total = total + (came[n] if after is None else lax.optimization_barrier((came[n], after))[0])
    return total


def solution(mesh):
    placed = (P("row", "col"), P("row", "col"), P("row", "col"))
    return jax.shard_map(
        local, mesh=mesh, in_specs=placed, out_specs=P(("row", "layer"), "col"), check_vma=False
    )
```
